32 devices in a mesh: sweep: 2 (over x), cell: 8 (over z, y), head: 2 (over core).
Axes of the slice: x: 2, y: 2, z: 4, core: 2. Of those that a mesh axis runs over, the one named last changes fastest.
Arguments:
- hidden: bfloat16 [4096, 8192], P(('sweep', 'cell'), 'head'), parts along dimension 0, may hold values from -6 to 6
- w_key: bfloat16 [8192, 512], P(None, 'head'), may hold values from -0.0625 to 0.0625
- w_value: bfloat16 [8192, 512], P(None, 'head'), may hold values from -0.0625 to 0.0625
- queries: bfloat16 [4096, 4096], P(('sweep', 'cell'), 'head'), parts along dimension 0, as said below
- span_order: int32 [16, 8], P(('sweep', 'cell')), parts along dimension 0, may hold values from 0 to 7, as said below
- span_count: int32 [16], P(('sweep', 'cell')), parts along dimension 0, may hold values from 2 to 8
- needle: int32 [16], P(('sweep', 'cell')), parts along dimension 0, may hold values from 0 to 7, as said below
- owners: int32 [8, 2], P('sweep'), parts along dimension 0, may hold values from 0 to 7, as said below
Outputs:
- attended: bfloat16 [4096, 4096], P(('sweep', 'cell'), 'head'), parts along dimension 0
The draws below stay inside these ranges and needn't reach their ends.
There are 2 independent parts, one for each index of `sweep`. The reference program is written for one: setup_inputs(seed, part) draws one part's arguments, and reference() takes and returns one part's arrays. A program takes and returns all parts, laid end to end along the dimension named above; an argument that names none is the same for every part. Nothing has to cross between parts.
Inputs may be any that keep to these rules, and one draw needn't show every extreme that they name: `span_order`: every row is a permutation of 0 to 7. `needle`: below the same cell's span_count. `owners`: all 8 entries of a part are distinct. `queries`: every entry lies in -64 to 64.
All inputs are finite; a program needn't handle non-finite values.
Results may differ from the reference program's by a relative error of at most 0.004.
The reference program's roundings to bfloat16 on the way count: a program that leaves them out, or rounds other values in their place, can miss the bound.
Values may be sent and summed in bfloat16 or wider, within the bound.
A program may use at most 128 MiB of HBM per device.

```python
import math
import jax
import jax.numpy as jnp
from jax import lax

D = 8192
HD = 128
KVH = 4
QH = 32
CH = 256
ROUNDS = 4
GROUP = 8
CELLS = 8
SLOTS = 8


def draw_queries(key, part):
    full_shape = (CELLS * CH, QH * HD)
    return jnp.clip(jax.random.normal(key, full_shape, jnp.float32), -6.0, 6.0).astype(jnp.bfloat16)


def cell_plan(key):
    base_key = jax.random.fold_in(key, 11)
    cell_keys = jax.random.split(jax.random.fold_in(base_key, 1), CELLS)
    cell_order = jax.vmap(lambda sub_key: jax.random.permutation(sub_key, SLOTS))(cell_keys).astype(jnp.int32)
    cell_ids = jnp.arange(CELLS, dtype=jnp.int32)
    full_cell = jax.random.randint(jax.random.fold_in(base_key, 2), (), 0, CELLS)
    short_cell = (full_cell + 1) % CELLS
    cell_count = jax.random.randint(jax.random.fold_in(base_key, 3), (CELLS,), 2, SLOTS + 1)
    cell_count = jnp.where(cell_ids == full_cell, SLOTS, jnp.where(cell_ids == short_cell, 2, cell_count)).astype(jnp.int32)
    needle_slot = jax.random.randint(jax.random.fold_in(base_key, 4), (CELLS,), 0, cell_count)
    needle_slot = jnp.where(cell_ids == full_cell, SLOTS - 1, needle_slot).astype(jnp.int32)
    return (cell_order, cell_count, needle_slot)


def draw_span_order(key, part):
    return cell_plan(key)[0]


def draw_span_count(key, part):
    return cell_plan(key)[1]


def draw_needle(key, part):
    return cell_plan(key)[2]


def draw_owners(key, part):
    shuffled = jax.random.permutation(jax.random.fold_in(key, 5), CELLS).astype(jnp.int32)
    target = jnp.argmax(shuffled == CELLS - 1)
    place = jax.random.randint(jax.random.fold_in(key, 6), (), 0, min(SLOTS, CELLS))
    moved = shuffled[place]
    shuffled = shuffled.at[target].set(moved).at[place].set(CELLS - 1)
    return shuffled[jnp.arange(SLOTS) % CELLS].reshape(ROUNDS, 2).astype(jnp.int32)


def steps_of(stream_key, dims, cuts, least, top_value):
    factor_of, own = 1.0, jax.random.fold_in(stream_key, 6)
    for axis_at, blocks in cuts:
        draws = jnp.exp(jax.random.uniform(jax.random.fold_in(own, axis_at), (blocks,), jnp.float32, least / len(cuts), top_value / len(cuts)))
        factor_of = factor_of * jnp.repeat(draws, dims[axis_at] // blocks).reshape([-1 if axis == axis_at else 1 for axis in range(len(dims))])
    return factor_of


def scatter_about(rng, extent, scale, bound, pieces=(), kind=jnp.bfloat16):
    result = jax.random.normal(rng, extent, jnp.float32) * scale
    if len(pieces) > 0:
        result = steps_of(rng, extent, pieces, -0.22, 0.18) * result
    return jnp.clip(result, min=-bound, max=bound).astype(kind)


def setup_inputs(seed: int = 0, part: int = 0) -> dict:
    key_list = jax.random.split(jax.random.key(seed), 9)
    part_splits = jax.random.split(jax.random.fold_in(key_list[8], part), 9)
    hidden = scatter_about(part_splits[0], (CELLS * CH, D), 1.0, 6.0, ((0, 8), (1, 2)))
    w_key = scatter_about(key_list[1], (D, KVH * HD), D ** -0.5, 0.0625, ((1, 2),))
    w_value = scatter_about(key_list[2], (D, KVH * HD), D ** -0.5, 0.0625, ((1, 2),))
    queries = draw_queries(jax.random.fold_in(jax.random.fold_in(key_list[8], part), 71), part)
    span_order = draw_span_order(jax.random.fold_in(jax.random.fold_in(key_list[8], part), 71), part)
    span_count = draw_span_count(jax.random.fold_in(jax.random.fold_in(key_list[8], part), 71), part)
    needle = draw_needle(jax.random.fold_in(jax.random.fold_in(key_list[8], part), 71), part)
    owners = draw_owners(jax.random.fold_in(jax.random.fold_in(key_list[8], part), 71), part)
    return dict(hidden=hidden, w_key=w_key, w_value=w_value, queries=queries, span_order=span_order, span_count=span_count, needle=needle, owners=owners)


rope_theta = 500000.0

def rotary(values, positions):
    half_dim = values.shape[-1] // 2
    frequency = rope_theta ** (-2.0 * jnp.arange(half_dim, dtype=jnp.float32) / values.shape[-1])
    angles = positions.astype(jnp.float32)[..., None] * frequency
    cosine = jnp.cos(angles)
    sine_part = jnp.sin(angles)
    first = values[..., :half_dim]
    second = values[..., half_dim:]
    return jnp.concatenate([first * cosine - second * sine_part, second * cosine + first * sine_part], axis=-1)

def reference(hidden, w_key, w_value, queries, span_order, span_count, needle, owners):
    key_rows = jnp.dot(hidden, w_key, preferred_element_type=jnp.float32).astype(jnp.bfloat16)
    value_rows = jnp.dot(hidden, w_value, preferred_element_type=jnp.float32).astype(jnp.bfloat16)
    slot_owner = owners.reshape(-1)
    slot_total = slot_owner.shape[0]
    context_keys = key_rows.reshape(CELLS, CH, KVH, HD)[slot_owner].astype(jnp.float32)
    context_values = value_rows.reshape(CELLS, CH, KVH, HD)[slot_owner].reshape(slot_total * CH, KVH, HD).astype(jnp.float32)
    lane_ids = jnp.arange(CH, dtype=jnp.int32)
    slot_ids = jnp.arange(slot_total, dtype=jnp.int32)
    score_scale = 1.0 / math.sqrt(HD)

    def one_cell(cell_item):
        query_rows, cell_order, cell_count, needle_slot = cell_item
        key_pos = cell_order[:, None] * CH + lane_ids[None, :]
        rot_keys = rotary(context_keys, key_pos[:, :, None]).astype(jnp.bfloat16)
        rot_keys = lax.optimization_barrier(rot_keys).astype(jnp.float32).reshape(slot_total * CH, KVH, HD)
        query_pos = cell_order[needle_slot] * CH + lane_ids
        rot_query = rotary(query_rows.reshape(CH, KVH, GROUP, HD).astype(jnp.float32), query_pos[:, None, None]).astype(jnp.bfloat16)
        rot_query = lax.optimization_barrier(rot_query).astype(jnp.float32)
        scores = jnp.einsum('ikgd,jkd->ikgj', rot_query, rot_keys) * score_scale
        before = (slot_ids < cell_count) & (cell_order < cell_order[needle_slot])
        causal = (slot_ids == needle_slot)[:, None, None] & (lane_ids[None, None, :] <= lane_ids[None, :, None])
        visible = jnp.transpose(before[:, None, None] | causal, (1, 0, 2)).reshape(CH, slot_total * CH)
        scores = jnp.where(visible[:, None, None, :], scores, -jnp.inf)
        running_max = lax.optimization_barrier(jnp.max(scores, axis=-1, keepdims=True))
        weights = jnp.exp(scores - running_max)
        weight_sum = lax.optimization_barrier(jnp.sum(weights, axis=-1))
        rounded = lax.optimization_barrier(weights.astype(jnp.bfloat16)).astype(jnp.float32)
        mixed_rows = jnp.einsum('ikgj,jkd->ikgd', rounded, context_values)
        return (mixed_rows / weight_sum[..., None]).astype(jnp.bfloat16).reshape(CH, QH * HD)
    outputs = lax.map(one_cell, (queries.reshape(CELLS, CH, QH * HD), span_order, span_count, needle))
    return outputs.reshape(CELLS * CH, QH * HD)
```

```python
import functools
import math

import jax
import jax.numpy as jnp
import numpy as np
from jax import lax
from jax.experimental import pallas as pl
from jax.experimental.pallas import tpu as pltpu
from jax.sharding import PartitionSpec as P

HD = 128
GROUP = 8
ROPE_THETA = 500000.0
MESH = pl.DeviceIdType.MESH
UP, DOWN, ACROSS, BACK = 0, 1, 2, 3


def grid_of(cells):
    fast = max(d for d in range(1, math.isqrt(cells) + 1) if cells % d == 0)
    return cells // fast, fast


def rope_tables(rows, slots):
    half = HD // 2
    frequency = (ROPE_THETA ** (-2.0 * np.arange(half) / HD)).astype(np.float32).astype(np.float64)
    frequency = np.concatenate([frequency, frequency])
    row_angle = np.arange(rows)[:, None] * frequency
    place_angle = (np.arange(slots) * rows)[:, None] * frequency
    return [
        np.asarray(t, np.float32)
        for t in (np.cos(row_angle), np.sin(row_angle), np.cos(place_angle), np.sin(place_angle))
    ]


def kernel(
    cells, heads, slots, depth_step,
    hidden, w_key, w_value, queries, order, count, needle, owners, cos_row, sin_row, cos_place, sin_place,
    out,
    own_hidden, far_hidden, key_w, value_w, key_sum, value_sum, q_rows, q_turned,
    kv, k_rot, bias, top, total, mixed,
    hid_sem, far_send, far_recv, kw_sem, vw_sem, q_sem, send_sem, recv_sem,
):
    rows = hidden.shape[0]
    half_depth = hidden.shape[1]
    pieces = half_depth // depth_step
    kv_heads = w_key.shape[1] // HD
    lines, columns = grid_of(cells)
    cell = lax.axis_index("cell")
    head = lax.axis_index("head")
    z = cell // columns
    y = cell % columns

    def at(zz, yy):
        return zz * columns + yy

    def hid_copy(c):
        cols = pl.ds(pl.multiple_of(c * depth_step, depth_step), depth_step)
        return pltpu.make_async_copy(hidden.at[:, cols], own_hidden.at[c], hid_sem.at[c])

    def weight_copy(source, target, sem, c):
        span = pl.ds(pl.multiple_of(c * depth_step, depth_step), depth_step)
        return pltpu.make_async_copy(source.at[span, :], target.at[c], sem.at[c])

    far = [lax.rem(head + step, heads) for step in range(1, heads)]
    for c in range(pieces):
        hid_copy(c).start()
        weight_copy(w_key, key_w, kw_sem, head * pieces + c).start()
        weight_copy(w_value, value_w, vw_sem, head * pieces + c).start()
    for step in range(1, heads):
        back = lax.rem(head + heads - step, heads)
        for c in range(pieces):
            weight_copy(w_key, key_w, kw_sem, back * pieces + c).start()
            weight_copy(w_value, value_w, vw_sem, back * pieces + c).start()
    q_copy = pltpu.make_async_copy(queries, q_rows, q_sem)
    q_copy.start()

    barrier = pltpu.get_barrier_semaphore()
    for other in far:
        pl.semaphore_signal(barrier, inc=1, device_id={"head": other}, device_id_type=MESH)
    exists = {UP: z + 1 < lines, DOWN: z >= 1, ACROSS: y + 1 < columns, BACK: y >= 1}
    target = {UP: cell + columns, DOWN: cell - columns, ACROSS: cell + 1, BACK: cell - 1}
    greeted = jnp.int32(heads - 1)
    for way in (UP, DOWN, ACROSS, BACK):
        greeted = greeted + exists[way].astype(jnp.int32)

        @pl.when(exists[way])
        def _():
            pl.semaphore_signal(barrier, inc=1, device_id={"cell": target[way]}, device_id_type=MESH)

    pl.semaphore_wait(barrier, greeted)

    def far_copy(step, c):
        cols = pl.ds(pl.multiple_of(c * depth_step, depth_step), depth_step)
        return pltpu.make_async_remote_copy(
            src_ref=hidden.at[:, cols], dst_ref=far_hidden.at[step - 1, c],
            send_sem=far_send.at[step - 1, c], recv_sem=far_recv.at[step - 1, c],
            device_id={"head": lax.rem(head + step, heads)}, device_id_type=MESH,
        )

    for step in range(1, heads):
        for c in range(pieces):
            far_copy(step, c).start()

    key_sum[...] = jnp.zeros_like(key_sum)
    value_sum[...] = jnp.zeros_like(value_sum)

    def own_piece(c, carry):
        hid_copy(c).wait()
        w = head * pieces + c
        weight_copy(w_key, key_w, kw_sem, w).wait()
        key_sum[...] += jnp.dot(own_hidden[c], key_w[w], preferred_element_type=jnp.float32)
        weight_copy(w_value, value_w, vw_sem, w).wait()
        value_sum[...] += jnp.dot(own_hidden[c], value_w[w], preferred_element_type=jnp.float32)
        return carry

    lax.fori_loop(0, pieces, own_piece, 0)
    for step in range(1, heads):
        back = lax.rem(head + heads - step, heads)

        def far_piece(c, carry):
            w = back * pieces + c
            far_copy(step, c).wait_recv()
            weight_copy(w_key, key_w, kw_sem, w).wait()
            key_sum[...] += jnp.dot(far_hidden[step - 1, c], key_w[w], preferred_element_type=jnp.float32)
            weight_copy(w_value, value_w, vw_sem, w).wait()
            value_sum[...] += jnp.dot(far_hidden[step - 1, c], value_w[w], preferred_element_type=jnp.float32)
            return carry

        lax.fori_loop(0, pieces, far_piece, 0)

    def shard_copy(way, part, source):
        return pltpu.make_async_remote_copy(
            src_ref=kv.at[part, source], dst_ref=kv.at[part, source],
            send_sem=send_sem.at[way, part, source], recv_sem=recv_sem.at[part, source],
            device_id={"cell": target[way]}, device_id_type=MESH,
        )

    def send(way, part, source, allowed, ending=False):
        @pl.when(allowed)
        def _():
            copy = shard_copy(way, part, source)
            copy.wait_send() if ending else copy.start()

    def arrived(part, source):
        pltpu.make_async_remote_copy(
            src_ref=kv.at[part, source], dst_ref=kv.at[part, source],
            send_sem=send_sem.at[UP, part, source], recv_sem=recv_sem.at[part, source],
            device_id={"cell": lax.rem(cell + 1, cells)}, device_id_type=MESH,
        ).wait_recv()

    kv[0, cell] = key_sum[...].astype(jnp.bfloat16)
    for way in (UP, DOWN, ACROSS, BACK):
        send(way, 0, cell, exists[way])
    kv[1, cell] = value_sum[...].T.astype(jnp.bfloat16)
    for way in (UP, DOWN, ACROSS, BACK):
        send(way, 1, cell, exists[way])

    lane = lax.broadcasted_iota(jnp.int32, (rows, HD), 1)

    def turn_tables(place):
        cos_p = cos_place[pl.ds(place, 1), :]
        sin_p = sin_place[pl.ds(place, 1), :]
        cosine = cos_p * cos_row[...] - sin_p * sin_row[...]
        sine = sin_p * cos_row[...] + cos_p * sin_row[...]
        return cosine, jnp.where(lane < HD // 2, -sine, sine)

    def turned(values, cosine, sine):
        return values * cosine + pltpu.roll(values, HD // 2, 1) * sine

    needle_slot = needle[0]
    used = count[0]
    needle_place = jnp.int32(0)
    for s in range(slots):
        needle_place += jnp.where(needle_slot == s, order[0, s], 0)

    q_copy.wait()
    q_cos, q_sin = turn_tables(needle_place)

    def turn_query(h, carry):
        cols = pl.ds(pl.multiple_of(h * HD, HD), HD)
        row = turned(q_rows[:, cols].astype(jnp.float32), q_cos, q_sin)
        q_turned[h] = row.T.astype(jnp.bfloat16)
        top[h] = jnp.full(top.shape[1:], -1e30, jnp.float32)
        total[h] = jnp.zeros(total.shape[1:], jnp.float32)
        mixed[h] = jnp.zeros(mixed.shape[1:], jnp.float32)
        return carry

    lax.fori_loop(0, kv_heads * GROUP, turn_query, 0)
    exponent = math.log2(math.e) / math.sqrt(HD)

    def attend(source, slot, place):
        offset = jnp.where(
            slot == needle_slot, 0,
            jnp.where((slot >= 0) & (slot < used) & (place < needle_place), rows, -rows),
        )
        cosine, sine = turn_tables(place)
        for k in range(kv_heads):
            block = kv[0, source, :, k * HD:(k + 1) * HD].astype(jnp.float32)
            k_rot[k] = turned(block, cosine, sine).astype(jnp.bfloat16)
        ahead = lax.broadcasted_iota(jnp.int32, (rows, rows), 0) - lax.broadcasted_iota(
            jnp.int32, (rows, rows), 1
        )
        bias[...] = jnp.where(ahead <= offset, 0.0, -jnp.inf)
        for k in range(kv_heads):
            def one_head(g, carry):
                h = k * GROUP + g
                scores = jnp.dot(k_rot[k], q_turned[h], preferred_element_type=jnp.float32) + bias[...]
                before = top[h]
                now = jnp.maximum(before, jnp.max(scores, axis=0, keepdims=True))
                fade = jnp.exp2((before - now) * exponent)
                weights = jnp.exp2((scores - now) * exponent)
                top[h] = now
                total[h] = total[h] * fade + jnp.sum(weights, axis=0, keepdims=True)
                mixed[h] = mixed[h] * fade + jnp.dot(
                    kv[1, source, k * HD:(k + 1) * HD, :], weights.astype(jnp.bfloat16),
                    preferred_element_type=jnp.float32,
                )
                return carry

            lax.fori_loop(0, GROUP, one_head, 0, unroll=4)

    def slot_of(source):
        slot, place = jnp.int32(-1), jnp.int32(0)
        for s in range(slots):
            here = owners[s // 2, s % 2] == source
            slot = jnp.where(here, s, slot)
            place = jnp.where(here, order[0, s], place)
        return slot, place

    def line_round(distance, divert, ending=False):
        for part in (0, 1):
            for way, zz in ((DOWN, z + distance), (UP, z - distance)):
                here = (zz >= 0) & (zz < lines)
                source = at(jnp.clip(zz, 0, lines - 1), y)

                if not ending:
                    @pl.when(here)
                    def _():
                        arrived(part, source)

                send(way, part, source, here & exists[way], ending)
                if divert:
                    kept = ((z == 1) & (zz == 0)) | ((z == lines - 2) & (zz == lines - 1))
                    if part == 0:
                        kept = kept | ((z == 0) & (zz == 1)) | ((z == lines - 1) & (zz == lines - 2))
                    here = here & jnp.logical_not(kept)
                send(ACROSS, part, source, here & exists[ACROSS], ending)
                send(BACK, part, source, here & exists[BACK], ending)

    if cells == slots and columns == 2 and lines == 4:
        mirror = at(z, 1 - y)
        edge = (z == 0) | (z == lines - 1)

        def events(r, ending=False):
            line_round(r, True, ending)
            if r == 1:
                for part in (0, 1):
                    if not ending:
                        arrived(part, mirror)
                    send(UP, part, mirror, z == 0, ending)
                    send(DOWN, part, mirror, z == lines - 1, ending)
            if r == 2:
                send(DOWN, 0, mirror, z == 1, ending)
                send(UP, 0, mirror, z == lines - 2, ending)

        flip = z >= lines // 2
        near = jnp.where(flip, lines - 1 - z, z)
        edge_order = (0, 1, 4, 2, 6, 3, 7, 5)
        inner_order = (1, 0, 2, 5, 3, 4, 6, 7)

        def step(n, carry):
            for r, edge_at, inner_at in ((1, 1, 1), (2, 3, 4), (3, 4, 5)):
                @pl.when(n == jnp.where(near == 0, edge_at, inner_at))
                def _():
                    events(r)

            entry = jnp.int32(0)
            for i in range(2 * lines):
                entry = jnp.where(n == i, jnp.where(near == 0, edge_order[i], inner_order[i]), entry)
            mirrored = entry // lines
            zz = entry % lines
            zz = jnp.where(flip, lines - 1 - zz, zz)
            source = at(zz, jnp.where(mirrored == 1, 1 - y, y))

            @pl.when((mirrored == 1) & (zz != z))
            def _():
                arrived(0, source)
                arrived(1, source)

            slot, place = slot_of(source)
            attend(source, slot, place)
            return carry

        lax.fori_loop(0, 2 * lines, step, 0)
        for r in range(1, lines):
            events(r, True)
    else:
        for r in range(1, lines):
            line_round(r, False)
        for r in range(1, lines):
            line_round(r, False, True)

        def column_step(i, carry):
            distance = 1 + i // lines
            zz = i % lines
            for part in (0, 1):
                for way, yy in ((BACK, y + distance), (ACROSS, y - distance)):
                    here = (yy >= 0) & (yy < columns)
                    source = at(zz, jnp.clip(yy, 0, columns - 1))

                    @pl.when(here)
                    def _():
                        arrived(part, source)

                    @pl.when(here & exists[way])
                    def _():
                        shard_copy(way, part, source).start()
            return carry

        lax.fori_loop(0, (columns - 1) * lines, column_step, 0)

        def column_end(i, carry):
            distance = 1 + i // lines
            zz = i % lines
            for part in (0, 1):
                for way, yy in ((BACK, y + distance), (ACROSS, y - distance)):
                    @pl.when((yy >= 0) & (yy < columns) & exists[way])
                    def _():
                        shard_copy(way, part, at(zz, jnp.clip(yy, 0, columns - 1))).wait_send()
            return carry

        lax.fori_loop(0, (columns - 1) * lines, column_end, 0)

        def slot_step(s, carry):
            attend(owners[s // 2, s % 2], s, order[0, s])
            return carry

        lax.fori_loop(0, slots, slot_step, 0)

    def finish(h, carry):
        cols = pl.ds(pl.multiple_of(h * HD, HD), HD)
        out[:, cols] = (mixed[h] / total[h]).T.astype(jnp.bfloat16)
        return carry

    lax.fori_loop(0, kv_heads * GROUP, finish, 0)

    for step in range(1, heads):
        for c in range(pieces):
            far_copy(step, c).wait_send()
    for part in (0, 1):
        for way in (UP, DOWN, ACROSS, BACK):
            send(way, part, cell, exists[way], True)


def solution(mesh):
    cells, heads = mesh.shape["cell"], mesh.shape["head"]

    def on_device(hidden, w_key, w_value, queries, span_order, span_count, needle, owners):
        rows, half_depth = hidden.shape
        kv_columns = w_key.shape[1]
        kv_heads = kv_columns // HD
        q_heads = kv_heads * GROUP
        slots = span_order.shape[1]
        depth_step = 1024
        pieces = half_depth // depth_step
        tables = [jnp.asarray(t) for t in rope_tables(rows, slots)]
        anywhere = pl.BlockSpec(memory_space=pl.ANY)
        smem = pl.BlockSpec(memory_space=pltpu.SMEM)
        vmem = pl.BlockSpec(memory_space=pltpu.VMEM)
        dma = pltpu.SemaphoreType.DMA
        f32, bf16 = jnp.float32, jnp.bfloat16
        return pl.pallas_call(
            functools.partial(kernel, cells, heads, slots, depth_step),
            out_shape=jax.ShapeDtypeStruct((rows, q_heads * HD), bf16),
            in_specs=[anywhere] * 4 + [smem] * 4 + [vmem] * 4,
            out_specs=vmem,
            scratch_shapes=[
                pltpu.VMEM((pieces, rows, depth_step), bf16),
                pltpu.VMEM((heads - 1, pieces, rows, depth_step), bf16),
                pltpu.VMEM((heads * pieces, depth_step, kv_columns), bf16),
                pltpu.VMEM((heads * pieces, depth_step, kv_columns), bf16),
                pltpu.VMEM((rows, kv_columns), f32),
                pltpu.VMEM((rows, kv_columns), f32),
                pltpu.VMEM((rows, q_heads * HD), bf16),
                pltpu.VMEM((q_heads, HD, rows), bf16),
                pltpu.VMEM((2, cells, rows, kv_columns), bf16),
                pltpu.VMEM((kv_heads, rows, HD), bf16),
                pltpu.VMEM((rows, rows), f32),
                pltpu.VMEM((q_heads, 1, rows), f32),
                pltpu.VMEM((q_heads, 1, rows), f32),
                pltpu.VMEM((q_heads, HD, rows), f32),
                dma((pieces,)),
                dma((heads - 1, pieces)),
                dma((heads - 1, pieces)),
                dma((heads * pieces,)),
                dma((heads * pieces,)),
                dma,
                dma((4, 2, cells)),
                dma((2, cells)),
            ],
            compiler_params=pltpu.CompilerParams(
                collective_id=0, has_side_effects=True, vmem_limit_bytes=56 * 2**20
            ),
            name="span_attention",
        )(hidden, w_key, w_value, queries, span_order, span_count, needle, owners, *tables)

    in_specs = (
        P(("sweep", "cell"), "head"),
        P(None, "head"),
        P(None, "head"),
        P(("sweep", "cell"), "head"),
        P(("sweep", "cell"), None),
        P(("sweep", "cell")),
        P(("sweep", "cell")),
        P("sweep", None),
    )
    return jax.shard_map(
        on_device, mesh=mesh, in_specs=in_specs, out_specs=P(("sweep", "cell"), "head"), check_vma=False
    )
```

```python
import functools
import math

import jax
import jax.numpy as jnp
import numpy as np
from jax import lax
from jax.experimental import pallas as pl
from jax.experimental.pallas import tpu as pltpu
from jax.sharding import PartitionSpec as P

HD = 128
GROUP = 8
ROPE_THETA = 500000.0
MESH = pl.DeviceIdType.MESH
UP, DOWN, ACROSS, BACK = 0, 1, 2, 3
AHEAD, BEHIND = 2, 1


def grid_of(cells):
    fast = max(d for d in range(1, math.isqrt(cells) + 1) if cells % d == 0)
    return cells // fast, fast


def rope_tables(rows, slots):
    half = HD // 2
    frequency = (ROPE_THETA ** (-2.0 * np.arange(half) / HD)).astype(np.float32).astype(np.float64)
    frequency = np.concatenate([frequency, frequency])
    row_angle = np.arange(rows)[:, None] * frequency
    place_angle = (np.arange(slots) * rows)[:, None] * frequency
    return [
        np.asarray(t, np.float32)
        for t in (np.cos(row_angle), np.sin(row_angle), np.cos(place_angle), np.sin(place_angle))
    ]


def kernel(
    cells, heads, slots, depth_step,
    hidden, w_key, w_value, queries, order, count, needle, owners, cos_row, sin_row, cos_place, sin_place,
    out,
    own_hidden, far_hidden, key_w, value_w, key_sum, value_sum, q_rows, q_turned,
    kv, k_rot, bias, top, total, mixed,
    hid_sem, far_send, far_recv, kw_sem, vw_sem, q_sem, send_sem, recv_sem,
):
    rows = hidden.shape[0]
    half_depth = hidden.shape[1]
    pieces = half_depth // depth_step
    kv_heads = w_key.shape[1] // HD
    lines, columns = grid_of(cells)
    cell = lax.axis_index("cell")
    head = lax.axis_index("head")
    z = cell // columns
    y = cell % columns

    def at(zz, yy):
        return zz * columns + yy

    def hid_copy(c):
        cols = pl.ds(pl.multiple_of(c * depth_step, depth_step), depth_step)
        return pltpu.make_async_copy(hidden.at[:, cols], own_hidden.at[c], hid_sem.at[c])

    def weight_copy(source, target, sem, c):
        span = pl.ds(pl.multiple_of(c * depth_step, depth_step), depth_step)
        return pltpu.make_async_copy(source.at[span, :], target.at[c], sem.at[c])

    far = [lax.rem(head + step, heads) for step in range(1, heads)]
    for c in range(pieces):
        hid_copy(c).start()
        weight_copy(w_key, key_w, kw_sem, head * pieces + c).start()
        weight_copy(w_value, value_w, vw_sem, head * pieces + c).start()
    for step in range(1, heads):
        back = lax.rem(head + heads - step, heads)
        for c in range(pieces):
            weight_copy(w_key, key_w, kw_sem, back * pieces + c).start()
            weight_copy(w_value, value_w, vw_sem, back * pieces + c).start()
    q_copy = pltpu.make_async_copy(queries, q_rows, q_sem)
    q_copy.start()

    barrier = pltpu.get_barrier_semaphore()
    for other in far:
        pl.semaphore_signal(barrier, inc=1, device_id={"head": other}, device_id_type=MESH)
    exists = {UP: z + 1 < lines, DOWN: z >= 1, ACROSS: y + 1 < columns, BACK: y >= 1}
    target = {UP: cell + columns, DOWN: cell - columns, ACROSS: cell + 1, BACK: cell - 1}
    greeted = jnp.int32(heads - 1)
    for way in (UP, DOWN, ACROSS, BACK):
        greeted = greeted + exists[way].astype(jnp.int32)

        @pl.when(exists[way])
        def _():
            pl.semaphore_signal(barrier, inc=1, device_id={"cell": target[way]}, device_id_type=MESH)

    pl.semaphore_wait(barrier, greeted)

    def far_copy(step, c):
        cols = pl.ds(pl.multiple_of(c * depth_step, depth_step), depth_step)
        return pltpu.make_async_remote_copy(
            src_ref=hidden.at[:, cols], dst_ref=far_hidden.at[step - 1, c],
            send_sem=far_send.at[step - 1, c], recv_sem=far_recv.at[step - 1, c],
            device_id={"head": lax.rem(head + step, heads)}, device_id_type=MESH,
        )

    for step in range(1, heads):
        for c in range(pieces):
            far_copy(step, c).start()

    key_sum[...] = jnp.zeros_like(key_sum)
    value_sum[...] = jnp.zeros_like(value_sum)

    def own_piece(c, carry):
        hid_copy(c).wait()
        w = head * pieces + c
        weight_copy(w_key, key_w, kw_sem, w).wait()
        key_sum[...] += jnp.dot(own_hidden[c], key_w[w], preferred_element_type=jnp.float32)
        weight_copy(w_value, value_w, vw_sem, w).wait()
        value_sum[...] += jnp.dot(own_hidden[c], value_w[w], preferred_element_type=jnp.float32)
        return carry

    lax.fori_loop(0, pieces, own_piece, 0)
    for step in range(1, heads):
        back = lax.rem(head + heads - step, heads)

        def far_piece(c, carry):
            w = back * pieces + c
            far_copy(step, c).wait_recv()
            weight_copy(w_key, key_w, kw_sem, w).wait()
            key_sum[...] += jnp.dot(far_hidden[step - 1, c], key_w[w], preferred_element_type=jnp.float32)
            weight_copy(w_value, value_w, vw_sem, w).wait()
            value_sum[...] += jnp.dot(far_hidden[step - 1, c], value_w[w], preferred_element_type=jnp.float32)
            return carry

        lax.fori_loop(0, pieces, far_piece, 0)

    def shard_copy(way, part, source):
        return pltpu.make_async_remote_copy(
            src_ref=kv.at[part, source], dst_ref=kv.at[part, source],
            send_sem=send_sem.at[way, part, source], recv_sem=recv_sem.at[part, source],
            device_id={"cell": target[way]}, device_id_type=MESH,
        )

    def send(way, part, source, allowed, ending=False):
        @pl.when(allowed)
        def _():
            copy = shard_copy(way, part, source)
            copy.wait_send() if ending else copy.start()

    def arrived(part, source):
        pltpu.make_async_remote_copy(
            src_ref=kv.at[part, source], dst_ref=kv.at[part, source],
            send_sem=send_sem.at[UP, part, source], recv_sem=recv_sem.at[part, source],
            device_id={"cell": lax.rem(cell + 1, cells)}, device_id_type=MESH,
        ).wait_recv()

    kv[0, cell] = key_sum[...].astype(jnp.bfloat16)
    for way in (UP, DOWN, ACROSS, BACK):
        send(way, 0, cell, exists[way])
    kv[1, cell] = value_sum[...].T.astype(jnp.bfloat16)
    for way in (UP, DOWN, ACROSS, BACK):
        send(way, 1, cell, exists[way])

    lane = lax.broadcasted_iota(jnp.int32, (rows, HD), 1)

    def turn_tables(place):
        cos_p = cos_place[pl.ds(place, 1), :]
        sin_p = sin_place[pl.ds(place, 1), :]
        cosine = cos_p * cos_row[...] - sin_p * sin_row[...]
        sine = sin_p * cos_row[...] + cos_p * sin_row[...]
        return cosine, jnp.where(lane < HD // 2, -sine, sine)

    def turned(values, cosine, sine):
        return values * cosine + pltpu.roll(values, HD // 2, 1) * sine

    needle_slot = needle[0]
    used = count[0]
    needle_place = jnp.int32(0)
    for s in range(slots):
        needle_place += jnp.where(needle_slot == s, order[0, s], 0)

    q_copy.wait()
    q_cos, q_sin = turn_tables(needle_place)

    def turn_query(h, carry):
        cols = pl.ds(pl.multiple_of(h * HD, HD), HD)
        row = turned(q_rows[:, cols].astype(jnp.float32), q_cos, q_sin)
        q_turned[h] = row.T.astype(jnp.bfloat16)
        top[h] = jnp.full(top.shape[1:], -1e30, jnp.float32)
        total[h] = jnp.zeros(total.shape[1:], jnp.float32)
        mixed[h] = jnp.zeros(mixed.shape[1:], jnp.float32)
        return carry

    lax.fori_loop(0, kv_heads * GROUP, turn_query, 0)
    exponent = math.log2(math.e) / math.sqrt(HD)

    def attend(source, slot, place):
        offset = jnp.where(
            slot == needle_slot, 0,
            jnp.where((slot >= 0) & (slot < used) & (place < needle_place), rows, -rows),
        )
        cosine, sine = turn_tables(place)
        for k in range(kv_heads):
            block = kv[0, source, :, k * HD:(k + 1) * HD].astype(jnp.float32)
            k_rot[k] = turned(block, cosine, sine).astype(jnp.bfloat16)
        ahead = lax.broadcasted_iota(jnp.int32, (rows, rows), 0) - lax.broadcasted_iota(
            jnp.int32, (rows, rows), 1
        )
        bias[...] = jnp.where(ahead <= offset, 0.0, -jnp.inf)
        def score(h):
            return jnp.dot(k_rot[h // GROUP], q_turned[h], preferred_element_type=jnp.float32) + bias[...]

        def mix(h, fade, weights):
            k = h // GROUP
            mixed[h] = mixed[h] * fade + jnp.dot(
                kv[1, source, k * HD:(k + 1) * HD, :], weights, preferred_element_type=jnp.float32
            )

        q_heads = kv_heads * GROUP
        olds = [(top[h], total[h]) for h in range(q_heads)]
        news, scored, pending = [], [score(h) for h in range(AHEAD)], []
        for h in range(q_heads):
            if h + AHEAD < q_heads:
                scored.append(score(h + AHEAD))
            scores = scored[h]
            before, summed = olds[h]
            now = jnp.maximum(before, jnp.max(scores, axis=0, keepdims=True))
            fade = jnp.exp2((before - now) * exponent)
            weights = jnp.exp2((scores - now) * exponent)
            news.append((now, summed * fade + jnp.sum(weights, axis=0, keepdims=True)))
            pending.append((h, fade, weights.astype(jnp.bfloat16)))
            if len(pending) > BEHIND:
                mix(*pending.pop(0))
        for item in pending:
            mix(*item)
        for h in range(q_heads):
            top[h], total[h] = news[h]

    def slot_of(source):
        slot, place = jnp.int32(-1), jnp.int32(0)
        for s in range(slots):
            here = owners[s // 2, s % 2] == source
            slot = jnp.where(here, s, slot)
            place = jnp.where(here, order[0, s], place)
        return slot, place

    def line_round(distance, divert, ending=False):
        for part in (0, 1):
            for way, zz in ((DOWN, z + distance), (UP, z - distance)):
                here = (zz >= 0) & (zz < lines)
                source = at(jnp.clip(zz, 0, lines - 1), y)

                if not ending:
                    @pl.when(here)
                    def _():
                        arrived(part, source)

                send(way, part, source, here & exists[way], ending)
                if divert:
                    kept = ((z == 1) & (zz == 0)) | ((z == lines - 2) & (zz == lines - 1))
                    if part == 0:
                        kept = kept | ((z == 0) & (zz == 1)) | ((z == lines - 1) & (zz == lines - 2))
                    here = here & jnp.logical_not(kept)
                send(ACROSS, part, source, here & exists[ACROSS], ending)
                send(BACK, part, source, here & exists[BACK], ending)

    if cells == slots and columns == 2 and lines == 4:
        mirror = at(z, 1 - y)
        edge = (z == 0) | (z == lines - 1)

        def events(r, ending=False):
            line_round(r, True, ending)
            if r == 1:
                for part in (0, 1):
                    if not ending:
                        arrived(part, mirror)
                    send(UP, part, mirror, z == 0, ending)
                    send(DOWN, part, mirror, z == lines - 1, ending)
            if r == 2:
                send(DOWN, 0, mirror, z == 1, ending)
                send(UP, 0, mirror, z == lines - 2, ending)

        flip = z >= lines // 2
        near = jnp.where(flip, lines - 1 - z, z)
        edge_order = (0, 1, 4, 2, 6, 3, 7, 5)
        inner_order = (1, 0, 2, 5, 3, 4, 6, 7)

        def step(n, carry):
            for r, edge_at, inner_at in ((1, 1, 1), (2, 3, 4), (3, 4, 5)):
                @pl.when(n == jnp.where(near == 0, edge_at, inner_at))
                def _():
                    events(r)

            entry = jnp.int32(0)
            for i in range(2 * lines):
                entry = jnp.where(n == i, jnp.where(near == 0, edge_order[i], inner_order[i]), entry)
            mirrored = entry // lines
            zz = entry % lines
            zz = jnp.where(flip, lines - 1 - zz, zz)
            source = at(zz, jnp.where(mirrored == 1, 1 - y, y))

            @pl.when((mirrored == 1) & (zz != z))
            def _():
                arrived(0, source)
                arrived(1, source)

            slot, place = slot_of(source)
            attend(source, slot, place)
            return carry

        lax.fori_loop(0, 2 * lines, step, 0)
        for r in range(1, lines):
            events(r, True)
    else:
        for r in range(1, lines):
            line_round(r, False)
        for r in range(1, lines):
            line_round(r, False, True)

        def column_step(i, carry):
            distance = 1 + i // lines
            zz = i % lines
            for part in (0, 1):
                for way, yy in ((BACK, y + distance), (ACROSS, y - distance)):
                    here = (yy >= 0) & (yy < columns)
                    source = at(zz, jnp.clip(yy, 0, columns - 1))

                    @pl.when(here)
                    def _():
                        arrived(part, source)

                    @pl.when(here & exists[way])
                    def _():
                        shard_copy(way, part, source).start()
            return carry

        lax.fori_loop(0, (columns - 1) * lines, column_step, 0)

        def column_end(i, carry):
            distance = 1 + i // lines
            zz = i % lines
            for part in (0, 1):
                for way, yy in ((BACK, y + distance), (ACROSS, y - distance)):
                    @pl.when((yy >= 0) & (yy < columns) & exists[way])
                    def _():
                        shard_copy(way, part, at(zz, jnp.clip(yy, 0, columns - 1))).wait_send()
            return carry

        lax.fori_loop(0, (columns - 1) * lines, column_end, 0)

        def slot_step(s, carry):
            attend(owners[s // 2, s % 2], s, order[0, s])
            return carry

        lax.fori_loop(0, slots, slot_step, 0)

    def finish(h, carry):
        cols = pl.ds(pl.multiple_of(h * HD, HD), HD)
        out[:, cols] = (mixed[h] / total[h]).T.astype(jnp.bfloat16)
        return carry

    lax.fori_loop(0, kv_heads * GROUP, finish, 0)

    for step in range(1, heads):
        for c in range(pieces):
            far_copy(step, c).wait_send()
    for part in (0, 1):
        for way in (UP, DOWN, ACROSS, BACK):
            send(way, part, cell, exists[way], True)


def solution(mesh):
    cells, heads = mesh.shape["cell"], mesh.shape["head"]

    def on_device(hidden, w_key, w_value, queries, span_order, span_count, needle, owners):
        rows, half_depth = hidden.shape
        kv_columns = w_key.shape[1]
        kv_heads = kv_columns // HD
        q_heads = kv_heads * GROUP
        slots = span_order.shape[1]
        depth_step = 2048
        pieces = half_depth // depth_step
        tables = [jnp.asarray(t) for t in rope_tables(rows, slots)]
        anywhere = pl.BlockSpec(memory_space=pl.ANY)
        smem = pl.BlockSpec(memory_space=pltpu.SMEM)
        vmem = pl.BlockSpec(memory_space=pltpu.VMEM)
        dma = pltpu.SemaphoreType.DMA
        f32, bf16 = jnp.float32, jnp.bfloat16
        return pl.pallas_call(
            functools.partial(kernel, cells, heads, slots, depth_step),
            out_shape=jax.ShapeDtypeStruct((rows, q_heads * HD), bf16),
            in_specs=[anywhere] * 4 + [smem] * 4 + [vmem] * 4,
            out_specs=vmem,
            scratch_shapes=[
                pltpu.VMEM((pieces, rows, depth_step), bf16),
                pltpu.VMEM((heads - 1, pieces, rows, depth_step), bf16),
                pltpu.VMEM((heads * pieces, depth_step, kv_columns), bf16),
                pltpu.VMEM((heads * pieces, depth_step, kv_columns), bf16),
                pltpu.VMEM((rows, kv_columns), f32),
                pltpu.VMEM((rows, kv_columns), f32),
                pltpu.VMEM((rows, q_heads * HD), bf16),
                pltpu.VMEM((q_heads, HD, rows), bf16),
                pltpu.VMEM((2, cells, rows, kv_columns), bf16),
                pltpu.VMEM((kv_heads, rows, HD), bf16),
                pltpu.VMEM((rows, rows), f32),
                pltpu.VMEM((q_heads, 1, rows), f32),
                pltpu.VMEM((q_heads, 1, rows), f32),
                pltpu.VMEM((q_heads, HD, rows), f32),
                dma((pieces,)),
                dma((heads - 1, pieces)),
                dma((heads - 1, pieces)),
                dma((heads * pieces,)),
                dma((heads * pieces,)),
                dma,
                dma((4, 2, cells)),
                dma((2, cells)),
            ],
            compiler_params=pltpu.CompilerParams(
                collective_id=0, has_side_effects=True, vmem_limit_bytes=56 * 2**20
            ),
            name="span_attention",
        )(hidden, w_key, w_value, queries, span_order, span_count, needle, owners, *tables)

    in_specs = (
        P(("sweep", "cell"), "head"),
        P(None, "head"),
        P(None, "head"),
        P(("sweep", "cell"), "head"),
        P(("sweep", "cell"), None),
        P(("sweep", "cell")),
        P(("sweep", "cell")),
        P("sweep", None),
    )
    return jax.shard_map(
        on_device, mesh=mesh, in_specs=in_specs, out_specs=P(("sweep", "cell"), "head"), check_vma=False
    )
```
